256 devices in a mesh: grp: 4 (over z_hi), seq: 32 (over y, x, core), mp: 2 (over z_lo).
Axes of the slice: x: 4, y: 4, z: 8 (z_hi: 4, z_lo: 2; z = z_hi * 2 + z_lo), core: 2. Of those that a mesh axis runs over, the one named last changes fastest.
Arguments:
- queries: bfloat16 [4, 8192, 2048], P('grp', 'seq', 'mp'), may hold values from -400 to 400
- neighbours: bfloat16 [4, 128, 256, 1024], P('grp', 'seq'), may hold values from -6 to 6
- w_key: bfloat16 [1024, 2048], P(('grp', 'seq'), 'mp'), may hold values from -0.1875 to 0.1875
- w_value: bfloat16 [1024, 2048], P(('grp', 'seq'), 'mp'), may hold values from -0.1875 to 0.1875
- lambdas: float32 [16], P('mp'), may hold values from 0.2 to 0.9
- gain: float32 [2048], P('mp'), may hold values from 0.5 to 1.5
- counts: int32 [4], P('grp'), may hold values from 2 to 128, as said below
- d_out: bfloat16 [4, 8192, 2048], P('grp', 'seq', 'mp'), may hold values from -6 to 6
Outputs:
- attended: bfloat16 [4, 8192, 2048], P('grp', 'seq', 'mp')
- d_neigh: float32 [4, 128, 256, 1024], P('grp', 'seq', None, 'mp')
The draws below stay inside these ranges and needn't reach their ends.
Inputs may be any that keep to these rules, and one draw needn't show every extreme that they name: `counts`: at least one sequence has all 128 groups valid.
All inputs are finite; a program needn't handle non-finite values.
Results may differ from the reference program's by a relative error of at most 0.017.
Values may be sent and summed in bfloat16 or wider, within the bound.
No kernel may reach another device: no remote copies, remote signals or barrier semaphores. Data moves between devices by JAX's collectives and lax.ppermute only.
A program may use at most 128 MiB of HBM per device.

```python
import jax
import jax.numpy as jnp
from jax import lax

D_ENC = 1024
PAIRS = 16
KDIM = 64
VDIM = 128
GROUP = 64
NEIGH = 2
NLEN = 128
SEQS = 4
GROUPS = 128
TOKENS = 8192


def draw_queries(key, part):
    extent = (SEQS, TOKENS, PAIRS * 2 * KDIM)
    key_base = jax.random.fold_in(key, 11)
    sample = jax.random.truncated_normal(key_base, -6.0, 6.0, extent, jnp.float32)
    return sample.astype(jnp.bfloat16)


def draw_counts(key, part):
    key_base = jax.random.fold_in(key, 21)
    key_full = jax.random.fold_in(key, 22)
    ragged = jax.random.randint(key_base, (SEQS,), 2, GROUPS + 1, jnp.int32)
    full_seq = jax.random.randint(key_full, (), 0, SEQS, jnp.int32)
    which = jnp.arange(SEQS, dtype=jnp.int32)
    return jnp.where(which == full_seq, jnp.int32(GROUPS), ragged).astype(jnp.int32)


def steps_of(own_key, shape, cuts, least, high):
    factor_of, own = 1.0, jax.random.fold_in(own_key, 6)
    for dim, blocks in cuts:
        heights = jnp.exp(jax.random.uniform(jax.random.fold_in(own, dim), (blocks,), jnp.float32, least / len(cuts), high / len(cuts)))
        factor_of = factor_of * jnp.repeat(heights, shape[dim] // blocks).reshape([-1 if axis == dim else 1 for axis in range(len(shape))])
    return factor_of


def bell_draw(key, dims, spread, limit, shards=(), held_as=jnp.bfloat16):
    factor_of = steps_of(key, dims, shards, -0.22, 0.18) if shards else 1.0
    result = jax.random.normal(key, dims, jnp.float32) * spread * factor_of
    return jnp.minimum(jnp.maximum(result, -limit), limit).astype(held_as)


def setup_inputs(seed: int = 0) -> dict:
    keys = jax.random.split(jax.random.key(seed), 9)
    queries = draw_queries(jax.random.fold_in(keys[8], 71), 0)
    neighbours = bell_draw(keys[1], (SEQS, GROUPS, NEIGH * NLEN, D_ENC), 1.0, 6.0, ((0, 4), (1, 32)))
    w_key = bell_draw(keys[2], (D_ENC, PAIRS * 2 * KDIM), D_ENC ** -0.5, 0.1875, ((0, 128), (1, 2)))
    w_value = bell_draw(keys[3], (D_ENC, PAIRS * VDIM), D_ENC ** -0.5, 0.1875, ((0, 128), (1, 2)))
    lambdas = jnp.clip(0.2 + 0.7 * jax.random.uniform(keys[4], (PAIRS,), jnp.float32) ** steps_of(keys[4], (PAIRS,), ((0, 2),), -0.2, 0.2), 0.2, 0.9)
    gain = jnp.clip(1.0 + 0.1 * jax.random.normal(keys[5], (PAIRS * VDIM,), jnp.float32), 0.5, 1.5)
    counts = draw_counts(jax.random.fold_in(keys[8], 71), 0)
    d_out = bell_draw(keys[7], (SEQS, TOKENS, PAIRS * VDIM), 1.0, 6.0, ((0, 4), (1, 32), (2, 2)))
    return dict(queries=queries, neighbours=neighbours, w_key=w_key, w_value=w_value, lambdas=lambdas, gain=gain, counts=counts, d_out=d_out)


epsilon = 1e-06

def reference(queries, neighbours, w_key, w_value, lambdas, gain, counts, d_out):
    row_count = NEIGH * NLEN
    rows_all = GROUPS * row_count
    score_scale = KDIM ** (-0.5)
    gain_heads = gain.reshape(PAIRS, VDIM)
    lambda_b = lambdas[None, :, None, None]

    def one_sequence(items):
        encoded, query_rows, grad_rows, valid_count = items
        flat_enc = encoded.reshape(rows_all, D_ENC)
        key_own = jnp.dot(flat_enc, w_key, preferred_element_type=jnp.float32)
        value_own = jnp.dot(flat_enc, w_value, preferred_element_type=jnp.float32).astype(jnp.bfloat16)
        key_own = key_own.reshape(GROUPS, row_count, PAIRS, 2, KDIM)
        value_own = value_own.reshape(GROUPS, row_count, PAIRS, VDIM)
        key_heads = jnp.concatenate([jnp.zeros_like(key_own[:1]), key_own[:-1]], axis=0).astype(jnp.float32)
        value_heads = jnp.concatenate([jnp.zeros_like(value_own[:1]), value_own[:-1]], axis=0).astype(jnp.float32)
        query_heads = query_rows.reshape(GROUPS, GROUP, PAIRS, 2, KDIM).astype(jnp.float32)
        position = jnp.arange(GROUPS, dtype=jnp.int32)
        active = ((position >= 1) & (position < valid_count)).astype(jnp.float32)[:, None, None, None]
        scores = jnp.einsum('cqhmd,crhmd->chmqr', query_heads, key_heads, precision=lax.Precision.HIGHEST) * score_scale
        soft_maps = jax.nn.softmax(scores, axis=-1)
        mixed_w = (soft_maps[:, :, 0] - lambda_b * soft_maps[:, :, 1]).astype(jnp.bfloat16)
        heads = jnp.einsum('chqr,crhv->cqhv', mixed_w.astype(jnp.float32), value_heads)
        inverse = lax.rsqrt(lax.optimization_barrier(jnp.mean(heads * heads, axis=-1, keepdims=True)) + epsilon)
        normed = heads * inverse
        attended = (normed * gain_heads * active).astype(jnp.bfloat16).reshape(TOKENS, PAIRS * VDIM)
        upstream = grad_rows.reshape(GROUPS, GROUP, PAIRS, VDIM).astype(jnp.float32) * active
        d_normed = upstream * gain_heads
        d_heads = (inverse * (d_normed - normed * lax.optimization_barrier(jnp.mean(d_normed * normed, axis=-1, keepdims=True)))).astype(jnp.bfloat16)
        d_heads = d_heads.astype(jnp.float32)
        d_mixed = jnp.einsum('cqhv,crhv->chqr', d_heads, value_heads)
        d_values = jnp.einsum('chqr,cqhv->crhv', mixed_w.astype(jnp.float32), d_heads).astype(jnp.bfloat16)
        d_probs = jnp.stack([d_mixed, -lambda_b * d_mixed], axis=2)
        d_scores = (score_scale * soft_maps * (d_probs - lax.optimization_barrier(jnp.sum(d_probs * soft_maps, axis=-1, keepdims=True)))).astype(jnp.bfloat16)
        d_keys = jnp.einsum('chmqr,cqhmd->crhmd', d_scores.astype(jnp.float32), query_heads).astype(jnp.bfloat16)
        d_slots = jnp.dot(d_keys.reshape(rows_all, PAIRS * 2 * KDIM), w_key.T, preferred_element_type=jnp.float32)
        d_slots = d_slots + jnp.dot(d_values.reshape(rows_all, PAIRS * VDIM), w_value.T, preferred_element_type=jnp.float32)
        d_slots = d_slots.reshape(GROUPS, row_count, D_ENC)
        d_enc = jnp.concatenate([d_slots[1:], jnp.zeros_like(d_slots[:1])], axis=0)
        return (attended, d_enc)
    attended, d_neigh = lax.map(one_sequence, (neighbours, queries, d_out, counts))
    return (attended, d_neigh)
```

```python
import functools

import jax
import jax.numpy as jnp
from jax import lax
from jax.experimental import pallas as pl
from jax.experimental.pallas import tpu as pltpu
from jax.sharding import PartitionSpec as P

EPSILON = 1e-06
F32 = jnp.float32
BF16 = jnp.bfloat16

SIDE = 4
RELATIVE = (0, 1, -1, 2)


def seq_index(y, x, core):
    return ((y % SIDE) * SIDE + x % SIDE) * 2 + core


def chips():
    return [(y, x, core) for y in range(SIDE) for x in range(SIDE) for core in range(2)]


def other_core():
    return [(seq_index(y, x, c), seq_index(y, x, 1 - c)) for y, x, c in chips()]


def along(first, step):
    pairs = []
    for y, x, c in chips():
        on_x = (c == 0) == first
        target = seq_index(y, x + step, c) if on_x else seq_index(y + step, x, c)
        pairs.append((seq_index(y, x, c), target))
    return pairs


def dot(left, right, dims):
    return lax.dot_general(left, right, (dims, ((), ())), preferred_element_type=F32)


NN = ((1,), (0,))
NT = ((1,), (1,))
TN = ((0,), (0,))


def assemble_kernel(where, *refs):
    pieces, whole = refs[:-1], refs[-1]
    my_z, my_y, my_x, core = where[0], where[1], where[2], where[3]
    count = len(RELATIVE)
    for index, piece in enumerate(pieces):
        origin = core if index < count else 1 - core
        late = RELATIVE[index % count]
        for j, early in enumerate(RELATIVE):
            dx = jnp.where(origin == 0, early, late)
            dy = jnp.where(origin == 0, late, early)
            x = lax.rem(my_x - dx + SIDE, SIDE)
            y = lax.rem(my_y - dy + SIDE, SIDE)
            for k, flip in enumerate((0, 1, 3, 2)):
                z = my_z ^ flip
                row = pl.multiple_of(z * 256 + (y * SIDE + x) * 16, 16)
                whole[origin, pl.ds(row, 16), :] = piece[j * SIDE + k]


def assemble(where, pieces):
    rows = len(RELATIVE) ** 3 * 16
    cols = pieces[0].shape[-1]
    vmem = pl.BlockSpec(memory_space=pltpu.VMEM)
    return pl.pallas_call(
        assemble_kernel,
        out_shape=jax.ShapeDtypeStruct((2, rows, cols), BF16),
        in_specs=[pl.BlockSpec(memory_space=pltpu.SMEM)] + [vmem] * len(pieces),
        out_specs=vmem,
        compiler_params=pltpu.CompilerParams(vmem_limit_bytes=20 * 1024 * 1024),
        cost_estimate=pl.CostEstimate(flops=0, bytes_accessed=4 * rows * cols * 2, transcendentals=0),
    )(where, *pieces)


def group_kernel(
    info, lambdas, enc, weights, query, upstream, gain, attended, sent, kept, d_proj,
    *, pairs, head_dim, value_dim, tokens
):
    half = info[0]
    active = info[1].astype(F32)
    rows, width = enc.shape
    duo_cols = 4 * head_dim
    duo_vals = 2 * value_dim
    key_cols = pairs * 2 * head_dim
    encoded = enc[...]
    lane = lax.broadcasted_iota(jnp.int32, (2 * tokens, duo_cols), 1) // head_dim
    of_second = lax.broadcasted_iota(jnp.int32, (2 * tokens, duo_cols), 0) // tokens
    lane_second = lax.broadcasted_iota(jnp.int32, (1, 2 * tokens), 1) >= tokens
    for duo in range(pairs // 2):
        key_at = slice(duo * duo_cols, (duo + 1) * duo_cols)
        val_at = slice(duo * duo_vals, (duo + 1) * duo_vals)
        keys = dot(encoded, weights[0, :, key_at], NN)
        vals = dot(encoded, weights[1, :, val_at], NN).astype(BF16)
        high = keys.astype(BF16)
        rest = keys - high.astype(F32)
        middle = rest.astype(BF16)
        low = (rest - middle.astype(F32)).astype(BF16)
        duo_q = query[:, key_at]
        stacked = jnp.concatenate([duo_q, duo_q], axis=0)
        lam = jnp.where(lane_second, lambdas[2 * duo + 1], lambdas[2 * duo])
        probs, spread = [], []
        for m in range(2):
            q_of_map = jnp.where(lane == 2 * of_second + m, stacked, jnp.zeros_like(stacked))
            spread.append(q_of_map)
            scores = dot(high, q_of_map, NT) + (dot(middle, q_of_map, NT) + dot(low, q_of_map, NT))
            grown = jnp.exp(scores - jnp.max(scores, axis=0, keepdims=True))
            probs.append(grown * (1.0 / jnp.sum(grown, axis=0, keepdims=True)))
        mix = (probs[0] - lam * probs[1]).astype(BF16)
        both = dot(mix, vals, TN)
        d_rows = []
        for p in range(2):
            at = slice(duo * duo_vals + p * value_dim, duo * duo_vals + (p + 1) * value_dim)
            heads = both[p * tokens:(p + 1) * tokens, p * value_dim:(p + 1) * value_dim]
            inverse = lax.rsqrt(jnp.mean(heads * heads, axis=-1, keepdims=True) + EPSILON)
            normed = heads * inverse
            pair_gain = gain[:, at]
            attended[:, at] = (normed * pair_gain * active).astype(BF16)
            d_normed = upstream[:, at].astype(F32) * active * pair_gain
            d_heads = inverse * (d_normed - normed * jnp.mean(d_normed * normed, axis=-1, keepdims=True))
            d_heads = d_heads.astype(BF16)
            empty = jnp.zeros_like(d_heads)
            d_rows.append(jnp.concatenate([d_heads, empty] if p == 0 else [empty, d_heads], axis=1))
        d_both = jnp.concatenate(d_rows, axis=0)
        d_mix = dot(vals, d_both, NT)
        d_proj[:, key_cols + duo * duo_vals:key_cols + (duo + 1) * duo_vals] = dot(mix, d_both, NN).astype(BF16)
        d_scores = []
        for m in range(2):
            inner = jnp.sum(d_mix * probs[m], axis=0, keepdims=True)
            d_score = probs[m] * (d_mix - inner)
            d_scores.append((d_score if m == 0 else -lam * d_score).astype(BF16))
        d_proj[:, key_at] = dot(
            jnp.concatenate(d_scores, axis=1), jnp.concatenate(spread, axis=0), NN
        ).astype(BF16)
    half_width = width // 2
    for target, which in ((sent, 1 - half), (kept, half)):
        at = pl.ds(pl.multiple_of(which * half_width, half_width), half_width)
        total = dot(d_proj[:, :key_cols], weights[0, at, :], NT)
        total = total + dot(d_proj[:, key_cols:], weights[1, at, :], NT)
        target[...] = total.astype(target.dtype)


def one_group(info, lambdas, enc, weights, query, upstream, gain):
    rows, width = enc.shape
    tokens, key_cols = query.shape
    pairs = lambdas.shape[0]
    val_cols = gain.shape[1]
    vmem = pl.BlockSpec(memory_space=pltpu.VMEM)
    smem = pl.BlockSpec(memory_space=pltpu.SMEM)
    kernel = functools.partial(
        group_kernel, pairs=pairs, head_dim=key_cols // (2 * pairs), value_dim=val_cols // pairs, tokens=tokens
    )
    flops = 4 * rows * width * (key_cols + val_cols) + 14 * rows * tokens * val_cols
    return pl.pallas_call(
        kernel,
        out_shape=(
            jax.ShapeDtypeStruct((tokens, val_cols), BF16),
            jax.ShapeDtypeStruct((rows, width // 2), BF16),
            jax.ShapeDtypeStruct((rows, width // 2), F32),
        ),
        in_specs=[smem, smem, vmem, vmem, vmem, vmem, vmem],
        out_specs=(vmem, vmem, vmem),
        scratch_shapes=[pltpu.VMEM((rows, key_cols + val_cols), BF16)],
        compiler_params=pltpu.CompilerParams(vmem_limit_bytes=24 * 1024 * 1024),
        cost_estimate=pl.CostEstimate(flops=flops, bytes_accessed=6 * 1024 * 1024, transcendentals=2 * rows * tokens * pairs),
    )(info, lambdas, enc, weights, query, upstream, gain)


def swap(value, axis, flip):
    count = lax.axis_size(axis)
    return lax.ppermute(value, axis, [(i, i ^ flip) for i in range(count)])


def gather_weights(w_key, w_value):
    core = lax.axis_index("seq") % 2
    first = core == 0
    own = jnp.where(first, w_key, w_value)
    got = lax.ppermute(jnp.where(first, w_value, w_key), "seq", other_core())
    rows = jnp.where(first, jnp.concatenate([own, got], axis=0), jnp.concatenate([got, own], axis=0))[None]
    for flip in (1, 3):
        rows = jnp.concatenate([rows, swap(rows, "grp", flip)], axis=0)
    early = [rows] + [lax.ppermute(rows, "seq", along(True, step)) for step in RELATIVE[1:]]
    block = jnp.concatenate(early, axis=0)
    late = [block] + [lax.ppermute(block, "seq", along(False, step)) for step in RELATIVE[1:]]
    swapped = [lax.ppermute(piece, "seq", other_core()) for piece in late]
    return late + swapped


def on_device(queries, neighbours, w_key, w_value, lambdas, gain, counts, d_out):
    group_count = neighbours.shape[1]
    pair_count = lambdas.shape[0]
    group_len = queries.shape[1] // group_count
    head_dim = w_key.shape[1] // (2 * pair_count)
    seq_count = lax.axis_size("seq")
    seq = lax.axis_index("seq")
    half = lax.axis_index("mp")
    where = jnp.stack([lax.axis_index("grp"), seq // (2 * SIDE), (seq // 2) % SIDE, seq % 2]).astype(jnp.int32)

    first_tokens = jnp.concatenate([queries[0, :group_len], d_out[0, :group_len]], axis=1)
    coming = lax.ppermute(first_tokens, "seq", [(i, (i - 1) % seq_count) for i in range(seq_count)])
    weights = assemble(where, gather_weights(w_key, w_value))

    scale = jnp.asarray(head_dim ** (-0.5), BF16)
    cols = queries.shape[2]
    gains = gain[None]
    received, kept, attended = {}, {}, {}
    for group in [group_count - 1] + list(range(group_count - 1)):
        if group == group_count - 1:
            query, upstream = coming[:, :cols], coming[:, cols:]
        else:
            at = slice((group + 1) * group_len, (group + 2) * group_len)
            query, upstream = queries[0, at], d_out[0, at]
        position = seq * group_count + group + 1
        active = (position >= 1) & (position < counts[0])
        info = jnp.stack([half, active.astype(jnp.int32)]).astype(jnp.int32)
        attended[group], sent, kept[group] = one_group(
            info, lambdas, neighbours[0, group], weights, query * scale, upstream, gains
        )
        received[group] = swap(sent, "mp", 1)
        if group == group_count - 1:
            attended[group] = lax.ppermute(
                attended[group], "seq", [(i, (i + 1) % seq_count) for i in range(seq_count)]
            )
    d_neigh = jnp.stack([kept[g] + received[g].astype(F32) for g in range(group_count)])
    order = [group_count - 1] + list(range(group_count - 1))
    return (jnp.concatenate([attended[g] for g in order], axis=0)[None], d_neigh[None])


def solution(mesh):
    in_specs = (
        P("grp", "seq", "mp"),
        P("grp", "seq", None, None),
        P(("grp", "seq"), "mp"),
        P(("grp", "seq"), "mp"),
        P("mp"),
        P("mp"),
        P("grp"),
        P("grp", "seq", "mp"),
    )
    out_specs = (P("grp", "seq", "mp"), P("grp", "seq", None, "mp"))
    return jax.shard_map(
        on_device, mesh=mesh, in_specs=in_specs, out_specs=out_specs, check_vma=False
    )
```

```python
import functools

import jax
import jax.numpy as jnp
import numpy as np
from jax import lax
from jax.experimental import pallas as pl
from jax.experimental.pallas import tpu as pltpu
from jax.sharding import PartitionSpec as P

EPSILON = 1e-06
F32 = jnp.float32
BF16 = jnp.bfloat16

SIDE = 4
RELATIVE = (0, 1, -1, 2)


def seq_index(y, x, core):
    return ((y % SIDE) * SIDE + x % SIDE) * 2 + core


def chips():
    return [(y, x, core) for y in range(SIDE) for x in range(SIDE) for core in range(2)]


def other_core():
    return [(seq_index(y, x, c), seq_index(y, x, 1 - c)) for y, x, c in chips()]


def along(first, step):
    pairs = []
    for y, x, c in chips():
        on_x = (c == 0) == first
        target = seq_index(y, x + step, c) if on_x else seq_index(y + step, x, c)
        pairs.append((seq_index(y, x, c), target))
    return pairs


def dot(left, right, dims):
    return lax.dot_general(left, right, (dims, ((), ())), preferred_element_type=F32)


NN = ((1,), (0,))
NT = ((1,), (1,))
TN = ((0,), (0,))


def assemble_kernel(info, *refs, places):
    whole = refs[-1]
    my_z, my_y, my_x, core = info[0], info[1], info[2], info[3]
    for (swapped, late), piece in zip(places, refs):
        origin = 1 - core if swapped else core
        for j, early in enumerate(RELATIVE):
            dx = jnp.where(origin == 0, early, late)
            dy = jnp.where(origin == 0, late, early)
            x = lax.rem(my_x - dx + SIDE, SIDE)
            y = lax.rem(my_y - dy + SIDE, SIDE)
            for k, flip in enumerate((0, 1, 3, 2)):
                z = my_z ^ flip
                row = pl.multiple_of(z * 256 + (y * SIDE + x) * 16, 16)
                whole[origin, pl.ds(row, 16), :] = piece[j * SIDE + k]


def assemble(info, pieces, places, whole=None):
    rows = len(RELATIVE) ** 3 * 16
    cols = pieces[0].shape[-1]
    vmem = pl.BlockSpec(memory_space=pltpu.VMEM)
    earlier = [] if whole is None else [whole]
    return pl.pallas_call(
        functools.partial(assemble_kernel, places=places),
        out_shape=jax.ShapeDtypeStruct((2, rows, cols), BF16),
        in_specs=[pl.BlockSpec(memory_space=pltpu.SMEM)] + [vmem] * (len(pieces) + len(earlier)),
        out_specs=vmem,
        input_output_aliases={1 + len(pieces): 0} if earlier else {},
        compiler_params=pltpu.CompilerParams(vmem_limit_bytes=20 * 1024 * 1024),
        cost_estimate=pl.CostEstimate(flops=0, bytes_accessed=8 * rows * cols, transcendentals=0),
    )(info, *pieces, *earlier)


def group_kernel(
    info, lambdas, states, weights, mask, queries, cotangents, gain, attended, sent, d_proj,
    *, group, query_at, token_at, pairs, head_dim, value_dim, tokens
):
    half = info[4]
    position = info[5] + (group + 1)
    active = jnp.where((position >= 1) & (position < info[6]), 1.0, 0.0)
    width = states.shape[3]
    duo_cols = 4 * head_dim
    duo_vals = 2 * value_dim
    key_cols = pairs * 2 * head_dim
    encoded = states[0, group]
    query = queries.at[query_at]
    upstream = cotangents.at[token_at]
    lane_second = lax.broadcasted_iota(jnp.int32, (1, 2 * tokens), 1) >= tokens
    duos = range(pairs // 2)
    key_at = [slice(duo * duo_cols, (duo + 1) * duo_cols) for duo in duos]
    val_at = [slice(duo * duo_vals, (duo + 1) * duo_vals) for duo in duos]
    lam = [jnp.where(lane_second, lambdas[2 * duo + 1], lambdas[2 * duo]) for duo in duos]
    vals, spread, scores, probs, mix, both, d_both, d_mix = {}, {}, {}, {}, {}, {}, {}, {}
    for duo in duos:
        keys = dot(encoded, weights[0, :, key_at[duo]], NN)
        vals[duo] = dot(encoded, weights[1, :, val_at[duo]], NN).astype(BF16)
        high = keys.astype(BF16)
        rest = keys - high.astype(F32)
        middle = rest.astype(BF16)
        low = (rest - middle.astype(F32)).astype(BF16)
        duo_q = query[:, key_at[duo]]
        spread[duo] = jnp.concatenate([duo_q] * 4, axis=0) * mask[...]
        for m in range(2):
            q_of_map = spread[duo][2 * tokens * m:2 * tokens * (m + 1)]
            scores[duo, m] = dot(high, q_of_map, NT) + (dot(middle, q_of_map, NT) + dot(low, q_of_map, NT))
    for duo in duos:
        for m in range(2):
            grown = jnp.exp(scores[duo, m] - jnp.max(scores[duo, m], axis=0, keepdims=True))
            probs[duo, m] = grown * (1.0 / jnp.sum(grown, axis=0, keepdims=True))
        mix[duo] = (probs[duo, 0] - lam[duo] * probs[duo, 1]).astype(BF16)
    for duo in duos:
        both[duo] = dot(mix[duo], vals[duo], TN)
    for duo in duos:
        d_rows = []
        for p in range(2):
            at = slice(duo * duo_vals + p * value_dim, duo * duo_vals + (p + 1) * value_dim)
            heads = both[duo][p * tokens:(p + 1) * tokens, p * value_dim:(p + 1) * value_dim]
            inverse = lax.rsqrt(jnp.mean(heads * heads, axis=-1, keepdims=True) + EPSILON)
            normed = heads * inverse
            pair_gain = gain[:, at]
            attended[:, at] = (normed * pair_gain * active).astype(BF16)
            d_normed = upstream[:, at].astype(F32) * active * pair_gain
            d_heads = inverse * (d_normed - normed * jnp.mean(d_normed * normed, axis=-1, keepdims=True))
            d_heads = d_heads.astype(BF16)
            empty = jnp.zeros_like(d_heads)
            d_rows.append(jnp.concatenate([d_heads, empty] if p == 0 else [empty, d_heads], axis=1))
        d_both[duo] = jnp.concatenate(d_rows, axis=0)
    for duo in duos:
        d_mix[duo] = dot(vals[duo], d_both[duo], NT)
        d_proj[:, key_cols + duo * duo_vals:key_cols + (duo + 1) * duo_vals] = dot(mix[duo], d_both[duo], NN).astype(BF16)
    for duo in duos:
        d_scores = []
        for m in range(2):
            inner = jnp.sum(d_mix[duo] * probs[duo, m], axis=0, keepdims=True)
            d_score = probs[duo, m] * (d_mix[duo] - inner)
            d_scores.append((d_score if m == 0 else -lam[duo] * d_score).astype(BF16))
        d_proj[:, key_at[duo]] = dot(
            jnp.concatenate(d_scores, axis=1), spread[duo], NN
        ).astype(BF16)
    half_width = width // 2
    at = pl.ds(pl.multiple_of((1 - half) * half_width, half_width), half_width)
    sent[...] = back_projected(d_proj, weights, at, key_cols).astype(BF16)


def back_projected(d_proj, weights, at, key_cols):
    return dot(d_proj[:, :key_cols], weights[0, at, :], NT) + dot(d_proj[:, key_cols:], weights[1, at, :], NT)


def query_mask(tokens, head_dim):
    row = np.arange(4 * tokens)[:, None]
    m, p = row // (2 * tokens), row // tokens % 2
    lane = np.arange(4 * head_dim)[None] // head_dim
    return jnp.asarray(np.where(lane == 2 * p + m, head_dim ** (-0.5), 0.0), BF16)


def one_group(info, lambdas, states, weights, mask, queries, cotangents, gain, *, group, query_at, token_at, tokens):
    rows, width = states.shape[2:]
    val_cols = gain.shape[1]
    pairs = lambdas.shape[0]
    head_dim = mask.shape[1] // 4
    key_cols = 2 * pairs * head_dim
    vmem = pl.BlockSpec(memory_space=pltpu.VMEM)
    smem = pl.BlockSpec(memory_space=pltpu.SMEM)
    kernel = functools.partial(
        group_kernel, group=group, query_at=query_at, token_at=token_at, pairs=pairs, head_dim=head_dim,
        value_dim=val_cols // pairs, tokens=tokens,
    )
    flops = 3 * rows * width * (key_cols + val_cols) + 14 * rows * tokens * val_cols
    return pl.pallas_call(
        kernel,
        out_shape=(
            jax.ShapeDtypeStruct((tokens, val_cols), BF16),
            jax.ShapeDtypeStruct((rows, width // 2), BF16),
            jax.ShapeDtypeStruct((rows, key_cols + val_cols), BF16),
        ),
        in_specs=[smem, smem, vmem, vmem, vmem, vmem, vmem, vmem],
        out_specs=(vmem, vmem, vmem),
        compiler_params=pltpu.CompilerParams(vmem_limit_bytes=12 * 1024 * 1024),
        cost_estimate=pl.CostEstimate(
            flops=4 * flops, bytes_accessed=6 * 1024 * 1024, transcendentals=2 * rows * tokens * pairs
        ),
    )(info, lambdas, states, weights, mask, queries, cotangents, gain)


def own_half_kernel(info, weights, *refs, count, key_cols):
    d_proj, received, (d_neigh, share) = refs[:count], refs[count:2 * count - 1], refs[2 * count - 1:]
    width = share.shape[1]
    at = pl.ds(pl.multiple_of(info[4] * width, width), width)
    for group in range(count - 1):
        @pl.when(pl.program_id(0) == group)
        def _():
            if group == 0:
                share[...] = back_projected(d_proj[count - 1], weights, at, key_cols)
            d_neigh[0, 0] = back_projected(d_proj[group], weights, at, key_cols) + received[group][...].astype(F32)


def own_half(info, weights, d_proj, received, order):
    count = len(d_proj)
    rows, width = received[0].shape
    vmem = pl.BlockSpec(memory_space=pltpu.VMEM)

    def place(step):
        group = 0
        for index, value in enumerate(order):
            group = jnp.where(step == index, value, group)
        return 0, group, 0, 0

    return pl.pallas_call(
        functools.partial(own_half_kernel, count=count, key_cols=weights.shape[2]),
        grid=(count - 1,),
        out_shape=(jax.ShapeDtypeStruct((1, count, rows, width), F32), jax.ShapeDtypeStruct((rows, width), F32)),
        in_specs=[pl.BlockSpec(memory_space=pltpu.SMEM)] + [vmem] * (2 * count),
        out_specs=(pl.BlockSpec((1, 1, rows, width), place), vmem),
        compiler_params=pltpu.CompilerParams(vmem_limit_bytes=12 * 1024 * 1024),
        cost_estimate=pl.CostEstimate(flops=2 * count * rows * width * 2048, bytes_accessed=6 * 1024 * 1024, transcendentals=0),
    )(info, weights, *d_proj, *received)


def last_sum_kernel(share, received, earlier, d_neigh):
    del earlier
    d_neigh[0, 0] = share[...] + received[...].astype(F32)


def last_sum(share, received, d_neigh, group):
    rows, width = share.shape
    vmem = pl.BlockSpec(memory_space=pltpu.VMEM)
    return pl.pallas_call(
        last_sum_kernel,
        grid=(1,),
        out_shape=jax.ShapeDtypeStruct(d_neigh.shape, F32),
        in_specs=[vmem, vmem, pl.BlockSpec(memory_space=pl.ANY)],
        out_specs=pl.BlockSpec((1, 1, rows, width), lambda step: (0, group, 0, 0)),
        input_output_aliases={2: 0},
        compiler_params=pltpu.CompilerParams(vmem_limit_bytes=6 * 1024 * 1024),
    )(share, received, d_neigh)


def swap(value, axis, flip):
    count = lax.axis_size(axis)
    return lax.ppermute(value, axis, [(i, i ^ flip) for i in range(count)])


def gather_weights(info, w_key, w_value, prepare, raw):
    core = lax.axis_index("seq") % 2
    first = core == 0
    own = jnp.where(first, w_key, w_value)
    got = lax.ppermute(jnp.where(first, w_value, w_key), "seq", other_core())
    rows = jnp.where(first, jnp.concatenate([own, got], axis=0), jnp.concatenate([got, own], axis=0))[None]
    for flip in (1, 3):
        rows = jnp.concatenate([rows, swap(rows, "grp", flip)], axis=0)
    early = [rows] + [lax.ppermute(rows, "seq", along(True, step)) for step in RELATIVE[1:]]
    block = jnp.concatenate(early, axis=0)
    block, raw = lax.optimization_barrier((block, raw))
    late = [block] + [lax.ppermute(block, "seq", along(False, step)) for step in RELATIVE[1:]]
    late[-1], ready = lax.optimization_barrier((late[-1], prepare(*raw)))
    swapped = [lax.ppermute(piece, "seq", other_core()) for piece in late]
    places = tuple((0, late_at) for late_at in RELATIVE) + tuple((1, late_at) for late_at in RELATIVE)
    return assemble(info, late + swapped, places), ready


def on_device(queries, neighbours, w_key, w_value, lambdas, gain, counts, d_out):
    group_count = neighbours.shape[1]
    group_len = queries.shape[1] // group_count
    cols = queries.shape[2]
    head_dim = w_key.shape[1] // (2 * lambdas.shape[0])
    seq_count = lax.axis_size("seq")
    seq = lax.axis_index("seq")
    last = group_count - 1
    info = jnp.stack([
        lax.axis_index("grp"), seq // (2 * SIDE), (seq // 2) % SIDE, seq % 2, lax.axis_index("mp"),
        seq * group_count, counts[0],
    ]).astype(jnp.int32)

    def prepare(queries, d_out, gain):
        first_tokens = jnp.concatenate([queries[0, :group_len], d_out[0, :group_len]], axis=1)
        return first_tokens, gain[None]

    weights, (first_tokens, gains) = gather_weights(
        info, w_key, w_value, prepare, (queries, d_out, gain)
    )
    coming = lax.ppermute(first_tokens, "seq", [(i, (i - 1) % seq_count) for i in range(seq_count)])
    mask = query_mask(group_len, head_dim)
    attended, d_proj, received = [None] * group_count, [], []
    order = list(range(last - 1)) + [last, last - 1]
    turn = info
    for group in order:
        if group < last:
            own_rows = slice((group + 1) * group_len, (group + 2) * group_len)
            tokens_in = (queries, d_out)
            places = dict(query_at=(0, own_rows), token_at=(0, own_rows))
        else:
            tokens_in = (coming, coming)
            places = dict(query_at=(slice(None), slice(0, cols)), token_at=(slice(None), slice(cols, 2 * cols)))
        attended[group], sent, d_columns = one_group(
            turn, lambdas, neighbours, weights, mask, *tokens_in, gains, group=group, tokens=group_len, **places
        )
        d_proj.append(d_columns)
        received.append(swap(sent, "mp", 1))
        turn, d_proj[-1], coming = lax.optimization_barrier((turn, d_proj[-1], coming))
    first = lax.ppermute(attended[last], "seq", [(i, (i + 1) % seq_count) for i in range(seq_count)])
    d_neigh, share = own_half(info, weights, d_proj, received[:last], order)
    d_neigh = last_sum(share, received[last], d_neigh, order[last])
    return (jnp.concatenate([first] + attended[:last], axis=0)[None], d_neigh)


def solution(mesh):
    in_specs = (
        P("grp", "seq", "mp"),
        P("grp", "seq", None, None),
        P(("grp", "seq"), "mp"),
        P(("grp", "seq"), "mp"),
        P("mp"),
        P("mp"),
        P("grp"),
        P("grp", "seq", "mp"),
    )
    out_specs = (P("grp", "seq", "mp"), P("grp", "seq", None, "mp"))
    return jax.shard_map(
        on_device, mesh=mesh, in_specs=in_specs, out_specs=out_specs, check_vma=False
    )
```

```python
import functools

import jax
import jax.numpy as jnp
import numpy as np
from jax import lax
from jax.experimental import pallas as pl
from jax.experimental.pallas import tpu as pltpu
from jax.sharding import PartitionSpec as P

EPSILON = 1e-06
F32 = jnp.float32
BF16 = jnp.bfloat16

SIDE = 4
RELATIVE = (0, 1, -1, 2)


def seq_index(y, x, core):
    return ((y % SIDE) * SIDE + x % SIDE) * 2 + core


def chips():
    return [(y, x, core) for y in range(SIDE) for x in range(SIDE) for core in range(2)]


def other_core():
    return [(seq_index(y, x, c), seq_index(y, x, 1 - c)) for y, x, c in chips()]


def along(first, step):
    pairs = []
    for y, x, c in chips():
        on_x = (c == 0) == first
        target = seq_index(y, x + step, c) if on_x else seq_index(y + step, x, c)
        pairs.append((seq_index(y, x, c), target))
    return pairs


def dot(left, right, dims):
    return lax.dot_general(left, right, (dims, ((), ())), preferred_element_type=F32)


NN = ((1,), (0,))
NT = ((1,), (1,))
TN = ((0,), (0,))


def assemble_kernel(info, *refs, places):
    pieces, whole = refs[:-1], refs[-1]
    my_z, my_y, my_x, core = info[0], info[1], info[2], info[3]
    for piece, (swapped, steps) in zip(pieces, places):
        origin = 1 - core if swapped else core
        for j, (early, late) in enumerate(steps):
            dx = jnp.where(origin == 0, early, late)
            dy = jnp.where(origin == 0, late, early)
            x = lax.rem(my_x - dx + SIDE, SIDE)
            y = lax.rem(my_y - dy + SIDE, SIDE)
            for k, flip in enumerate((0, 1, 3, 2)):
                z = my_z ^ flip
                row = pl.multiple_of(z * 256 + (y * SIDE + x) * 16, 16)
                whole[origin, pl.ds(row, 16), :] = piece[j * SIDE + k]


def assemble(info, pieces, places, whole=None):
    rows = len(RELATIVE) ** 3 * 16
    cols = pieces[0].shape[-1]
    vmem = pl.BlockSpec(memory_space=pltpu.VMEM)
    earlier = [] if whole is None else [whole]
    return pl.pallas_call(
        functools.partial(assemble_kernel, places=places),
        out_shape=jax.ShapeDtypeStruct((2, rows, cols), BF16),
        in_specs=[pl.BlockSpec(memory_space=pltpu.SMEM)] + [vmem] * (len(pieces) + len(earlier)),
        out_specs=vmem,
        input_output_aliases={1 + len(pieces): 0} if earlier else {},
        compiler_params=pltpu.CompilerParams(vmem_limit_bytes=20 * 1024 * 1024),
        cost_estimate=pl.CostEstimate(flops=0, bytes_accessed=8 * rows * cols, transcendentals=0),
    )(info, *pieces, *earlier)


def group_kernel(
    info, lambdas, states, weights, mask, queries, cotangents, gain, attended, sent, d_proj,
    *, group, query_at, token_at, pairs, head_dim, value_dim, tokens
):
    half = info[4]
    position = info[5] + (group + 1)
    active = jnp.where((position >= 1) & (position < info[6]), 1.0, 0.0)
    width = states.shape[3]
    duo_cols = 4 * head_dim
    duo_vals = 2 * value_dim
    key_cols = pairs * 2 * head_dim
    encoded = states[0, group]
    query = queries.at[query_at]
    upstream = cotangents.at[token_at]
    lane_second = lax.broadcasted_iota(jnp.int32, (1, 2 * tokens), 1) >= tokens
    duos = range(pairs // 2)
    key_at = [slice(duo * duo_cols, (duo + 1) * duo_cols) for duo in duos]
    val_at = [slice(duo * duo_vals, (duo + 1) * duo_vals) for duo in duos]
    lam = [jnp.where(lane_second, lambdas[2 * duo + 1], lambdas[2 * duo]) for duo in duos]
    vals, spread, scores, probs, mix, both, d_both, d_mix = {}, {}, {}, {}, {}, {}, {}, {}
    for duo in duos:
        keys = dot(encoded, weights[0, :, key_at[duo]], NN)
        vals[duo] = dot(encoded, weights[1, :, val_at[duo]], NN).astype(BF16)
        high = keys.astype(BF16)
        rest = keys - high.astype(F32)
        middle = rest.astype(BF16)
        low = (rest - middle.astype(F32)).astype(BF16)
        duo_q = query[:, key_at[duo]]
        spread[duo] = jnp.concatenate([duo_q] * 4, axis=0) * mask[...]
        for m in range(2):
            q_of_map = spread[duo][2 * tokens * m:2 * tokens * (m + 1)]
            scores[duo, m] = dot(high, q_of_map, NT) + (dot(middle, q_of_map, NT) + dot(low, q_of_map, NT))
    for duo in duos:
        for m in range(2):
            grown = jnp.exp(scores[duo, m] - jnp.max(scores[duo, m], axis=0, keepdims=True))
            probs[duo, m] = grown * (1.0 / jnp.sum(grown, axis=0, keepdims=True))
        mix[duo] = (probs[duo, 0] - lam[duo] * probs[duo, 1]).astype(BF16)
    for duo in duos:
        both[duo] = dot(mix[duo], vals[duo], TN)
    for duo in duos:
        d_rows = []
        for p in range(2):
            at = slice(duo * duo_vals + p * value_dim, duo * duo_vals + (p + 1) * value_dim)
            heads = both[duo][p * tokens:(p + 1) * tokens, p * value_dim:(p + 1) * value_dim]
            inverse = lax.rsqrt(jnp.mean(heads * heads, axis=-1, keepdims=True) + EPSILON)
            normed = heads * inverse
            pair_gain = gain[:, at]
            attended[:, at] = (normed * pair_gain * active).astype(BF16)
            d_normed = upstream[:, at].astype(F32) * active * pair_gain
            d_heads = inverse * (d_normed - normed * jnp.mean(d_normed * normed, axis=-1, keepdims=True))
            d_heads = d_heads.astype(BF16)
            empty = jnp.zeros_like(d_heads)
            d_rows.append(jnp.concatenate([d_heads, empty] if p == 0 else [empty, d_heads], axis=1))
        d_both[duo] = jnp.concatenate(d_rows, axis=0)
    for duo in duos:
        d_mix[duo] = dot(vals[duo], d_both[duo], NT)
        d_proj[:, key_cols + duo * duo_vals:key_cols + (duo + 1) * duo_vals] = dot(mix[duo], d_both[duo], NN).astype(BF16)
    for duo in duos:
        d_scores = []
        for m in range(2):
            inner = jnp.sum(d_mix[duo] * probs[duo, m], axis=0, keepdims=True)
            d_score = probs[duo, m] * (d_mix[duo] - inner)
            d_scores.append((d_score if m == 0 else -lam[duo] * d_score).astype(BF16))
        d_proj[:, key_at[duo]] = dot(
            jnp.concatenate(d_scores, axis=1), spread[duo], NN
        ).astype(BF16)
    half_width = width // 2
    at = pl.ds(pl.multiple_of((1 - half) * half_width, half_width), half_width)
    sent[...] = back_projected(d_proj, weights, at, key_cols).astype(BF16)


def back_projected(d_proj, weights, at, key_cols):
    return dot(d_proj[:, :key_cols], weights[0, at, :], NT) + dot(d_proj[:, key_cols:], weights[1, at, :], NT)


def query_mask(tokens, head_dim):
    row = np.arange(4 * tokens)[:, None]
    m, p = row // (2 * tokens), row // tokens % 2
    lane = np.arange(4 * head_dim)[None] // head_dim
    return jnp.asarray(np.where(lane == 2 * p + m, head_dim ** (-0.5), 0.0), BF16)


def one_group(info, lambdas, states, weights, mask, queries, cotangents, gain, *, group, query_at, token_at, tokens):
    rows, width = states.shape[2:]
    val_cols = gain.shape[1]
    pairs = lambdas.shape[0]
    head_dim = mask.shape[1] // 4
    key_cols = 2 * pairs * head_dim
    vmem = pl.BlockSpec(memory_space=pltpu.VMEM)
    smem = pl.BlockSpec(memory_space=pltpu.SMEM)
    kernel = functools.partial(
        group_kernel, group=group, query_at=query_at, token_at=token_at, pairs=pairs, head_dim=head_dim,
        value_dim=val_cols // pairs, tokens=tokens,
    )
    flops = 3 * rows * width * (key_cols + val_cols) + 14 * rows * tokens * val_cols
    return pl.pallas_call(
        kernel,
        out_shape=(
            jax.ShapeDtypeStruct((tokens, val_cols), BF16),
            jax.ShapeDtypeStruct((rows, width // 2), BF16),
            jax.ShapeDtypeStruct((rows, key_cols + val_cols), BF16),
        ),
        in_specs=[smem, smem, vmem, vmem, vmem, vmem, vmem, vmem],
        out_specs=(vmem, vmem, vmem),
        compiler_params=pltpu.CompilerParams(vmem_limit_bytes=12 * 1024 * 1024),
        cost_estimate=pl.CostEstimate(
            flops=4 * flops, bytes_accessed=6 * 1024 * 1024, transcendentals=2 * rows * tokens * pairs
        ),
    )(info, lambdas, states, weights, mask, queries, cotangents, gain)


def own_half_kernel(info, weights, *refs, count, key_cols):
    d_proj, received, (d_neigh, share) = refs[:count], refs[count:2 * count - 1], refs[2 * count - 1:]
    width = share.shape[1]
    at = pl.ds(pl.multiple_of(info[4] * width, width), width)
    for group in range(count - 1):
        @pl.when(pl.program_id(0) == group)
        def _():
            if group == 0:
                share[...] = back_projected(d_proj[count - 1], weights, at, key_cols)
            d_neigh[0, 0] = back_projected(d_proj[group], weights, at, key_cols) + received[group][...].astype(F32)


def own_half(info, weights, d_proj, received, order):
    count = len(d_proj)
    rows, width = received[0].shape
    vmem = pl.BlockSpec(memory_space=pltpu.VMEM)

    def place(step):
        group = 0
        for index, value in enumerate(order):
            group = jnp.where(step == index, value, group)
        return 0, group, 0, 0

    return pl.pallas_call(
        functools.partial(own_half_kernel, count=count, key_cols=weights.shape[2]),
        grid=(count - 1,),
        out_shape=(jax.ShapeDtypeStruct((1, count, rows, width), F32), jax.ShapeDtypeStruct((rows, width), F32)),
        in_specs=[pl.BlockSpec(memory_space=pltpu.SMEM)] + [vmem] * (2 * count),
        out_specs=(pl.BlockSpec((1, 1, rows, width), place), vmem),
        compiler_params=pltpu.CompilerParams(vmem_limit_bytes=12 * 1024 * 1024),
        cost_estimate=pl.CostEstimate(flops=2 * count * rows * width * 2048, bytes_accessed=6 * 1024 * 1024, transcendentals=0),
    )(info, weights, *d_proj, *received)


def last_sum_kernel(share, received, earlier, d_neigh):
    del earlier
    d_neigh[0, 0] = share[...] + received[...].astype(F32)


def last_sum(share, received, d_neigh, group):
    rows, width = share.shape
    vmem = pl.BlockSpec(memory_space=pltpu.VMEM)
    return pl.pallas_call(
        last_sum_kernel,
        grid=(1,),
        out_shape=jax.ShapeDtypeStruct(d_neigh.shape, F32),
        in_specs=[vmem, vmem, pl.BlockSpec(memory_space=pl.ANY)],
        out_specs=pl.BlockSpec((1, 1, rows, width), lambda step: (0, group, 0, 0)),
        input_output_aliases={2: 0},
        compiler_params=pltpu.CompilerParams(vmem_limit_bytes=6 * 1024 * 1024),
    )(share, received, d_neigh)


def swap(value, axis, flip):
    count = lax.axis_size(axis)
    return lax.ppermute(value, axis, [(i, i ^ flip) for i in range(count)])


def gather_weights(info, w_key, w_value, prepare, raw):
    core = lax.axis_index("seq") % 2
    first = core == 0
    own = jnp.where(first, w_key, w_value)
    got = lax.ppermute(jnp.where(first, w_value, w_key), "seq", other_core())
    rows = jnp.where(first, jnp.concatenate([own, got], axis=0), jnp.concatenate([got, own], axis=0))[None]
    for flip in (1, 3):
        rows = jnp.concatenate([rows, swap(rows, "grp", flip)], axis=0)
    steps = RELATIVE[1:]
    early = [lax.ppermute(rows, "seq", along(True, step)) for step in steps]
    straight = [lax.ppermute(rows, "seq", along(False, step)) for step in steps]
    block = jnp.concatenate(early, axis=0)
    block, raw = lax.optimization_barrier((block, raw))
    late = [lax.ppermute(block, "seq", along(False, step)) for step in steps]
    late[-1], ready = lax.optimization_barrier((late[-1], prepare(*raw)))
    pieces = [jnp.concatenate([rows] + straight, axis=0), block] + late
    places = [[(0, step) for step in RELATIVE]] + [[(step, to) for step in steps] for to in RELATIVE]
    swapped = [lax.ppermute(piece, "seq", other_core()) for piece in pieces]
    order = [(0, place) for place in places] + [(1, place) for place in places]
    return assemble(info, pieces + swapped, order), ready


def on_device(queries, neighbours, w_key, w_value, lambdas, gain, counts, d_out):
    group_count = neighbours.shape[1]
    group_len = queries.shape[1] // group_count
    cols = queries.shape[2]
    head_dim = w_key.shape[1] // (2 * lambdas.shape[0])
    seq_count = lax.axis_size("seq")
    seq = lax.axis_index("seq")
    last = group_count - 1
    info = jnp.stack([
        lax.axis_index("grp"), seq // (2 * SIDE), (seq // 2) % SIDE, seq % 2, lax.axis_index("mp"),
        seq * group_count, counts[0],
    ]).astype(jnp.int32)

    def prepare(queries, d_out, gain):
        first_tokens = jnp.concatenate([queries[0, :group_len], d_out[0, :group_len]], axis=1)
        return first_tokens, gain[None]

    weights, (first_tokens, gains) = gather_weights(
        info, w_key, w_value, prepare, (queries, d_out, gain)
    )
    coming = lax.ppermute(first_tokens, "seq", [(i, (i - 1) % seq_count) for i in range(seq_count)])
    mask = query_mask(group_len, head_dim)
    attended, d_proj, received = [None] * group_count, [], []
    order = list(range(last - 1)) + [last, last - 1]
    turn = info
    for group in order:
        if group < last:
            own_rows = slice((group + 1) * group_len, (group + 2) * group_len)
            tokens_in = (queries, d_out)
            places = dict(query_at=(0, own_rows), token_at=(0, own_rows))
        else:
            tokens_in = (coming, coming)
            places = dict(query_at=(slice(None), slice(0, cols)), token_at=(slice(None), slice(cols, 2 * cols)))
        attended[group], sent, d_columns = one_group(
            turn, lambdas, neighbours, weights, mask, *tokens_in, gains, group=group, tokens=group_len, **places
        )
        d_proj.append(d_columns)
        received.append(swap(sent, "mp", 1))
        turn, d_proj[-1], coming = lax.optimization_barrier((turn, d_proj[-1], coming))
    first = lax.ppermute(attended[last], "seq", [(i, (i + 1) % seq_count) for i in range(seq_count)])
    d_neigh, share = own_half(info, weights, d_proj, received[:last], order)
    d_neigh = last_sum(share, received[last], d_neigh, order[last])
    return (jnp.concatenate([first] + attended[:last], axis=0)[None], d_neigh)


def solution(mesh):
    in_specs = (
        P("grp", "seq", "mp"),
        P("grp", "seq", None, None),
        P(("grp", "seq"), "mp"),
        P(("grp", "seq"), "mp"),
        P("mp"),
        P("mp"),
        P("grp"),
        P("grp", "seq", "mp"),
    )
    out_specs = (P("grp", "seq", "mp"), P("grp", "seq", None, "mp"))
    return jax.shard_map(
        on_device, mesh=mesh, in_specs=in_specs, out_specs=out_specs, check_vma=False
    )
```

```python
import functools

import jax
import jax.numpy as jnp
import numpy as np
from jax import lax
from jax.experimental import pallas as pl
from jax.experimental.pallas import tpu as pltpu
from jax.sharding import PartitionSpec as P

EPSILON = 1e-06
F32 = jnp.float32
BF16 = jnp.bfloat16

SIDE = 4
RELATIVE = (0, 1, -1, 2)


def seq_index(y, x, core):
    return ((y % SIDE) * SIDE + x % SIDE) * 2 + core


def chips():
    return [(y, x, core) for y in range(SIDE) for x in range(SIDE) for core in range(2)]


def other_core():
    return [(seq_index(y, x, c), seq_index(y, x, 1 - c)) for y, x, c in chips()]


def along(first, step):
    pairs = []
    for y, x, c in chips():
        on_x = (c == 0) == first
        target = seq_index(y, x + step, c) if on_x else seq_index(y + step, x, c)
        pairs.append((seq_index(y, x, c), target))
    return pairs


def dot(left, right, dims):
    return lax.dot_general(left, right, (dims, ((), ())), preferred_element_type=F32)


NN = ((1,), (0,))
NT = ((1,), (1,))
TN = ((0,), (0,))


def assemble_kernel(info, *refs, places):
    pieces, whole = refs[:-1], refs[-1]
    my_z, my_y, my_x, core = info[0], info[1], info[2], info[3]
    for piece, (swapped, steps) in zip(pieces, places):
        origin = 1 - core if swapped else core
        for j, (early, late) in enumerate(steps):
            dx = jnp.where(origin == 0, early, late)
            dy = jnp.where(origin == 0, late, early)
            x = lax.rem(my_x - dx + SIDE, SIDE)
            y = lax.rem(my_y - dy + SIDE, SIDE)
            for k, flip in enumerate((0, 1, 3, 2)):
                z = my_z ^ flip
                row = pl.multiple_of(z * 256 + (y * SIDE + x) * 16, 16)
                whole[origin, pl.ds(row, 16), :] = piece[j * SIDE + k]


def assemble(info, pieces, places, whole=None):
    rows = len(RELATIVE) ** 3 * 16
    cols = pieces[0].shape[-1]
    vmem = pl.BlockSpec(memory_space=pltpu.VMEM)
    earlier = [] if whole is None else [whole]
    return pl.pallas_call(
        functools.partial(assemble_kernel, places=places),
        out_shape=jax.ShapeDtypeStruct((2, rows, cols), BF16),
        in_specs=[pl.BlockSpec(memory_space=pltpu.SMEM)] + [vmem] * (len(pieces) + len(earlier)),
        out_specs=vmem,
        input_output_aliases={1 + len(pieces): 0} if earlier else {},
        compiler_params=pltpu.CompilerParams(vmem_limit_bytes=20 * 1024 * 1024),
        cost_estimate=pl.CostEstimate(flops=0, bytes_accessed=8 * rows * cols, transcendentals=0),
    )(info, *pieces, *earlier)


def group_kernel(
    info, lambdas, states, weights, mask, queries, cotangents, gain, attended, sent, d_proj,
    *, group, query_at, token_at, pairs, head_dim, value_dim, tokens
):
    half = info[4]
    position = info[5] + (group + 1)
    active = jnp.where((position >= 1) & (position < info[6]), 1.0, 0.0)
    width = states.shape[3]
    duo_cols = 4 * head_dim
    duo_vals = 2 * value_dim
    key_cols = pairs * 2 * head_dim
    encoded = states[0, group]
    query = queries.at[query_at]
    upstream = cotangents.at[token_at]
    lane_second = lax.broadcasted_iota(jnp.int32, (1, 2 * tokens), 1) >= tokens
    duos = range(pairs // 2)
    key_at = [slice(duo * duo_cols, (duo + 1) * duo_cols) for duo in duos]
    val_at = [slice(duo * duo_vals, (duo + 1) * duo_vals) for duo in duos]
    lam = [jnp.where(lane_second, lambdas[2 * duo + 1], lambdas[2 * duo]) for duo in duos]
    vals, spread, scores, probs, mix, both, d_both, d_mix = {}, {}, {}, {}, {}, {}, {}, {}
    def score_stage(duo):
        keys = dot(encoded, weights[0, :, key_at[duo]], NN)
        vals[duo] = dot(encoded, weights[1, :, val_at[duo]], NN).astype(BF16)
        high = keys.astype(BF16)
        rest = keys - high.astype(F32)
        middle = rest.astype(BF16)
        low = (rest - middle.astype(F32)).astype(BF16)
        duo_q = query[:, key_at[duo]]
        spread[duo] = jnp.concatenate([duo_q] * 4, axis=0) * mask[...]
        for m in range(2):
            q_of_map = spread[duo][2 * tokens * m:2 * tokens * (m + 1)]
            scores[duo, m] = dot(high, q_of_map, NT) + (dot(middle, q_of_map, NT) + dot(low, q_of_map, NT))

    def softmax_stage(duo):
        for m in range(2):
            grown = jnp.exp(scores[duo, m] - jnp.max(scores[duo, m], axis=0, keepdims=True))
            probs[duo, m] = grown * (1.0 / jnp.sum(grown, axis=0, keepdims=True))
        mix[duo] = (probs[duo, 0] - lam[duo] * probs[duo, 1]).astype(BF16)

    def heads_stage(duo):
        both[duo] = dot(mix[duo], vals[duo], TN)

    def norm_stage(duo):
        d_rows = []
        for p in range(2):
            at = slice(duo * duo_vals + p * value_dim, duo * duo_vals + (p + 1) * value_dim)
            heads = both[duo][p * tokens:(p + 1) * tokens, p * value_dim:(p + 1) * value_dim]
            inverse = lax.rsqrt(jnp.mean(heads * heads, axis=-1, keepdims=True) + EPSILON)
            normed = heads * inverse
            pair_gain = gain[:, at]
            attended[:, at] = (normed * pair_gain * active).astype(BF16)
            d_normed = upstream[:, at].astype(F32) * active * pair_gain
            d_heads = inverse * (d_normed - normed * jnp.mean(d_normed * normed, axis=-1, keepdims=True))
            d_heads = d_heads.astype(BF16)
            empty = jnp.zeros_like(d_heads)
            d_rows.append(jnp.concatenate([d_heads, empty] if p == 0 else [empty, d_heads], axis=1))
        d_both[duo] = jnp.concatenate(d_rows, axis=0)

    def d_mix_stage(duo):
        d_mix[duo] = dot(vals[duo], d_both[duo], NT)
        d_proj[:, key_cols + duo * duo_vals:key_cols + (duo + 1) * duo_vals] = dot(mix[duo], d_both[duo], NN).astype(BF16)

    def d_key_stage(duo):
        d_scores = []
        for m in range(2):
            inner = jnp.sum(d_mix[duo] * probs[duo, m], axis=0, keepdims=True)
            d_score = probs[duo, m] * (d_mix[duo] - inner)
            d_scores.append((d_score if m == 0 else -lam[duo] * d_score).astype(BF16))
        d_proj[:, key_at[duo]] = dot(
            jnp.concatenate(d_scores, axis=1), spread[duo], NN
        ).astype(BF16)

    stages = (score_stage, softmax_stage, heads_stage, norm_stage, d_mix_stage, d_key_stage)
    for step in range(len(duos) + len(stages) - 1):
        for behind, stage in enumerate(stages):
            if step - behind in duos:
                stage(step - behind)
    half_width = width // 2
    at = pl.ds(pl.multiple_of((1 - half) * half_width, half_width), half_width)
    sent[...] = back_projected(d_proj, weights, at, key_cols).astype(BF16)


def back_projected(d_proj, weights, at, key_cols):
    return dot(d_proj[:, :key_cols], weights[0, at, :], NT) + dot(d_proj[:, key_cols:], weights[1, at, :], NT)


def query_mask(tokens, head_dim):
    row = np.arange(4 * tokens)[:, None]
    m, p = row // (2 * tokens), row // tokens % 2
    lane = np.arange(4 * head_dim)[None] // head_dim
    return jnp.asarray(np.where(lane == 2 * p + m, head_dim ** (-0.5), 0.0), BF16)


def one_group(info, lambdas, states, weights, mask, queries, cotangents, gain, *, group, query_at, token_at, tokens):
    rows, width = states.shape[2:]
    val_cols = gain.shape[1]
    pairs = lambdas.shape[0]
    head_dim = mask.shape[1] // 4
    key_cols = 2 * pairs * head_dim
    vmem = pl.BlockSpec(memory_space=pltpu.VMEM)
    smem = pl.BlockSpec(memory_space=pltpu.SMEM)
    kernel = functools.partial(
        group_kernel, group=group, query_at=query_at, token_at=token_at, pairs=pairs, head_dim=head_dim,
        value_dim=val_cols // pairs, tokens=tokens,
    )
    flops = 3 * rows * width * (key_cols + val_cols) + 14 * rows * tokens * val_cols
    return pl.pallas_call(
        kernel,
        out_shape=(
            jax.ShapeDtypeStruct((tokens, val_cols), BF16),
            jax.ShapeDtypeStruct((rows, width // 2), BF16),
            jax.ShapeDtypeStruct((rows, key_cols + val_cols), BF16),
        ),
        in_specs=[smem, smem, vmem, vmem, vmem, vmem, vmem, vmem],
        out_specs=(vmem, vmem, vmem),
        compiler_params=pltpu.CompilerParams(vmem_limit_bytes=12 * 1024 * 1024),
        cost_estimate=pl.CostEstimate(
            flops=4 * flops, bytes_accessed=6 * 1024 * 1024, transcendentals=2 * rows * tokens * pairs
        ),
    )(info, lambdas, states, weights, mask, queries, cotangents, gain)


def own_half_kernel(info, weights, *refs, count, key_cols):
    d_proj, received, (d_neigh, share) = refs[:count], refs[count:2 * count - 1], refs[2 * count - 1:]
    width = share.shape[1]
    at = pl.ds(pl.multiple_of(info[4] * width, width), width)
    for group in range(count - 1):
        @pl.when(pl.program_id(0) == group)
        def _():
            if group == 0:
                share[...] = back_projected(d_proj[count - 1], weights, at, key_cols)
            d_neigh[0, 0] = back_projected(d_proj[group], weights, at, key_cols) + received[group][...].astype(F32)


def own_half(info, weights, d_proj, received, order):
    count = len(d_proj)
    rows, width = received[0].shape
    vmem = pl.BlockSpec(memory_space=pltpu.VMEM)

    def place(step):
        group = 0
        for index, value in enumerate(order):
            group = jnp.where(step == index, value, group)
        return 0, group, 0, 0

    return pl.pallas_call(
        functools.partial(own_half_kernel, count=count, key_cols=weights.shape[2]),
        grid=(count - 1,),
        out_shape=(jax.ShapeDtypeStruct((1, count, rows, width), F32), jax.ShapeDtypeStruct((rows, width), F32)),
        in_specs=[pl.BlockSpec(memory_space=pltpu.SMEM)] + [vmem] * (2 * count),
        out_specs=(pl.BlockSpec((1, 1, rows, width), place), vmem),
        compiler_params=pltpu.CompilerParams(vmem_limit_bytes=12 * 1024 * 1024),
        cost_estimate=pl.CostEstimate(flops=2 * count * rows * width * 2048, bytes_accessed=6 * 1024 * 1024, transcendentals=0),
    )(info, weights, *d_proj, *received)


def last_sum_kernel(share, received, earlier, d_neigh):
    del earlier
    d_neigh[0, 0] = share[...] + received[...].astype(F32)


def last_sum(share, received, d_neigh, group):
    rows, width = share.shape
    vmem = pl.BlockSpec(memory_space=pltpu.VMEM)
    return pl.pallas_call(
        last_sum_kernel,
        grid=(1,),
        out_shape=jax.ShapeDtypeStruct(d_neigh.shape, F32),
        in_specs=[vmem, vmem, pl.BlockSpec(memory_space=pl.ANY)],
        out_specs=pl.BlockSpec((1, 1, rows, width), lambda step: (0, group, 0, 0)),
        input_output_aliases={2: 0},
        compiler_params=pltpu.CompilerParams(vmem_limit_bytes=6 * 1024 * 1024),
    )(share, received, d_neigh)


def swap(value, axis, flip):
    count = lax.axis_size(axis)
    return lax.ppermute(value, axis, [(i, i ^ flip) for i in range(count)])


def gather_weights(info, w_key, w_value, prepare, raw):
    core = lax.axis_index("seq") & 1
    first = core == 0
    own = jnp.where(first, w_key, w_value)
    got = lax.ppermute(jnp.where(first, w_value, w_key), "seq", other_core())
    rows = jnp.where(first, jnp.concatenate([own, got], axis=0), jnp.concatenate([got, own], axis=0))[None]
    for flip in (1, 3):
        rows = jnp.concatenate([rows, swap(rows, "grp", flip)], axis=0)
    steps = RELATIVE[1:]
    early = [lax.ppermute(rows, "seq", along(True, step)) for step in steps]
    straight = [lax.ppermute(rows, "seq", along(False, step)) for step in steps]
    block = jnp.concatenate(early, axis=0)
    block, raw = lax.optimization_barrier((block, raw))
    late = [lax.ppermute(block, "seq", along(False, step)) for step in steps]
    late[-1], ready = lax.optimization_barrier((late[-1], prepare(*raw)))
    pieces = [jnp.concatenate([rows] + straight, axis=0), block] + late
    places = [[(0, step) for step in RELATIVE]] + [[(step, to) for step in steps] for to in RELATIVE]
    swapped = [lax.ppermute(piece, "seq", other_core()) for piece in pieces]
    order = [(0, place) for place in places] + [(1, place) for place in places]
    return assemble(info, pieces + swapped, order), ready


def on_device(queries, neighbours, w_key, w_value, lambdas, gain, counts, d_out):
    group_count = neighbours.shape[1]
    group_len = queries.shape[1] // group_count
    cols = queries.shape[2]
    head_dim = w_key.shape[1] // (2 * lambdas.shape[0])
    seq_count = lax.axis_size("seq")
    seq = lax.axis_index("seq")
    last = group_count - 1
    info = jnp.stack([
        lax.axis_index("grp"), lax.div(seq, 2 * SIDE), lax.rem(lax.div(seq, 2), SIDE), seq & 1, lax.axis_index("mp"),
        seq * group_count, counts[0],
    ]).astype(jnp.int32)

    def prepare(queries, d_out, gain):
        first_tokens = jnp.concatenate([queries[0, :group_len], d_out[0, :group_len]], axis=1)
        return first_tokens, gain[None]

    weights, (first_tokens, gains) = gather_weights(
        info, w_key, w_value, prepare, (queries, d_out, gain)
    )
    coming = lax.ppermute(first_tokens, "seq", [(i, (i - 1) % seq_count) for i in range(seq_count)])
    mask = query_mask(group_len, head_dim)
    attended, d_proj, received = [None] * group_count, [], []
    order = list(range(last - 1)) + [last, last - 1]
    turn = info
    for group in order:
        if group < last:
            own_rows = slice((group + 1) * group_len, (group + 2) * group_len)
            tokens_in = (queries, d_out)
            places = dict(query_at=(0, own_rows), token_at=(0, own_rows))
        else:
            tokens_in = (coming, coming)
            places = dict(query_at=(slice(None), slice(0, cols)), token_at=(slice(None), slice(cols, 2 * cols)))
        attended[group], sent, d_columns = one_group(
            turn, lambdas, neighbours, weights, mask, *tokens_in, gains, group=group, tokens=group_len, **places
        )
        d_proj.append(d_columns)
        received.append(swap(sent, "mp", 1))
        turn, d_proj[-1], coming = lax.optimization_barrier((turn, d_proj[-1], coming))
    first = lax.ppermute(attended[last], "seq", [(i, (i + 1) % seq_count) for i in range(seq_count)])
    d_neigh, share = own_half(info, weights, d_proj, received[:last], order)
    d_neigh = last_sum(share, received[last], d_neigh, order[last])
    return (jnp.concatenate([first] + attended[:last], axis=0)[None], d_neigh)


def solution(mesh):
    in_specs = (
        P("grp", "seq", "mp"),
        P("grp", "seq", None, None),
        P(("grp", "seq"), "mp"),
        P(("grp", "seq"), "mp"),
        P("mp"),
        P("mp"),
        P("grp"),
        P("grp", "seq", "mp"),
    )
    out_specs = (P("grp", "seq", "mp"), P("grp", "seq", None, "mp"))
    return jax.shard_map(
        on_device, mesh=mesh, in_specs=in_specs, out_specs=out_specs, check_vma=False
    )
```

```python
import functools

import jax
import jax.numpy as jnp
import numpy as np
from jax import lax
from jax.experimental import pallas as pl
from jax.experimental.pallas import tpu as pltpu
from jax.sharding import PartitionSpec as P

EPSILON = 1e-06
F32 = jnp.float32
BF16 = jnp.bfloat16

SIDE = 4
RELATIVE = (0, 1, -1, 2)


def seq_index(y, x, core):
    return ((y % SIDE) * SIDE + x % SIDE) * 2 + core


def chips():
    return [(y, x, core) for y in range(SIDE) for x in range(SIDE) for core in range(2)]


def other_core():
    return [(seq_index(y, x, c), seq_index(y, x, 1 - c)) for y, x, c in chips()]


def along(first, step):
    pairs = []
    for y, x, c in chips():
        on_x = (c == 0) == first
        target = seq_index(y, x + step, c) if on_x else seq_index(y + step, x, c)
        pairs.append((seq_index(y, x, c), target))
    return pairs


def dot(left, right, dims):
    return lax.dot_general(left, right, (dims, ((), ())), preferred_element_type=F32)


NN = ((1,), (0,))
NT = ((1,), (1,))
TN = ((0,), (0,))


def assemble_kernel(info, *refs, places):
    pieces, whole = refs[:-1], refs[-1]
    my_z, my_y, my_x, core = info[0], info[1], info[2], info[3]
    for piece, (swapped, steps) in zip(pieces, places):
        origin = 1 - core if swapped else core
        for j, (early, late) in enumerate(steps):
            dx = jnp.where(origin == 0, early, late)
            dy = jnp.where(origin == 0, late, early)
            x = lax.rem(my_x - dx + SIDE, SIDE)
            y = lax.rem(my_y - dy + SIDE, SIDE)
            for k, flip in enumerate((0, 1, 3, 2)):
                z = my_z ^ flip
                row = pl.multiple_of(z * 256 + (y * SIDE + x) * 16, 16)
                whole[origin, pl.ds(row, 16), :] = piece[j * SIDE + k]


def assemble(info, pieces, places, whole=None):
    rows = len(RELATIVE) ** 3 * 16
    cols = pieces[0].shape[-1]
    vmem = pl.BlockSpec(memory_space=pltpu.VMEM)
    earlier = [] if whole is None else [whole]
    return pl.pallas_call(
        functools.partial(assemble_kernel, places=places),
        out_shape=jax.ShapeDtypeStruct((2, rows, cols), BF16),
        in_specs=[pl.BlockSpec(memory_space=pltpu.SMEM)] + [vmem] * (len(pieces) + len(earlier)),
        out_specs=vmem,
        input_output_aliases={1 + len(pieces): 0} if earlier else {},
        compiler_params=pltpu.CompilerParams(vmem_limit_bytes=20 * 1024 * 1024),
        cost_estimate=pl.CostEstimate(flops=0, bytes_accessed=8 * rows * cols, transcendentals=0),
    )(info, *pieces, *earlier)


def group_kernel(
    info, lambdas, states, weights, mask, queries, cotangents, gain, attended, sent, d_proj,
    *, group, query_at, token_at, pairs, head_dim, value_dim, tokens
):
    half = info[4]
    position = info[5] + (group + 1)
    active = jnp.where((position >= 1) & (position < info[6]), 1.0, 0.0)
    width = states.shape[3]
    duo_cols = 4 * head_dim
    duo_vals = 2 * value_dim
    key_cols = pairs * 2 * head_dim
    encoded = states[0, group]
    query = queries.at[query_at]
    upstream = cotangents.at[token_at]
    lane_second = lax.broadcasted_iota(jnp.int32, (1, 2 * tokens), 1) >= tokens
    duos = range(pairs // 2)
    key_at = [slice(duo * duo_cols, (duo + 1) * duo_cols) for duo in duos]
    val_at = [slice(duo * duo_vals, (duo + 1) * duo_vals) for duo in duos]
    lam = [jnp.where(lane_second, lambdas[2 * duo + 1], lambdas[2 * duo]) for duo in duos]
    vals, spread, scores, probs, mix, both, d_both, d_mix = {}, {}, {}, {}, {}, {}, {}, {}
    def score_stage(duo):
        keys = dot(encoded, weights[0, :, key_at[duo]], NN)
        vals[duo] = dot(encoded, weights[1, :, val_at[duo]], NN).astype(BF16)
        high = keys.astype(BF16)
        rest = keys - high.astype(F32)
        middle = rest.astype(BF16)
        low = (rest - middle.astype(F32)).astype(BF16)
        parts = jnp.concatenate([high, middle, low], axis=1)
        duo_q = query[:, key_at[duo]]
        spread[duo] = jnp.concatenate([duo_q] * 4, axis=0) * mask[...]
        for m in range(2):
            q_of_map = spread[duo][2 * tokens * m:2 * tokens * (m + 1)]
            scores[duo, m] = dot(parts, jnp.concatenate([q_of_map] * 3, axis=1), NT)

    def softmax_stage(duo):
        for m in range(2):
            grown = jnp.exp(scores[duo, m] - jnp.max(scores[duo, m], axis=0, keepdims=True))
            probs[duo, m] = grown * (1.0 / jnp.sum(grown, axis=0, keepdims=True))
        mix[duo] = (probs[duo, 0] - lam[duo] * probs[duo, 1]).astype(BF16)

    def heads_stage(duo):
        both[duo] = dot(mix[duo], vals[duo], TN)

    def norm_stage(duo):
        d_rows = []
        for p in range(2):
            at = slice(duo * duo_vals + p * value_dim, duo * duo_vals + (p + 1) * value_dim)
            heads = both[duo][p * tokens:(p + 1) * tokens, p * value_dim:(p + 1) * value_dim]
            inverse = lax.rsqrt(jnp.mean(heads * heads, axis=-1, keepdims=True) + EPSILON)
            normed = heads * inverse
            pair_gain = gain[:, at]
            attended[:, at] = (normed * pair_gain * active).astype(BF16)
            d_normed = upstream[:, at].astype(F32) * active * pair_gain
            d_heads = inverse * (d_normed - normed * jnp.mean(d_normed * normed, axis=-1, keepdims=True))
            d_heads = d_heads.astype(BF16)
            empty = jnp.zeros_like(d_heads)
            d_rows.append(jnp.concatenate([d_heads, empty] if p == 0 else [empty, d_heads], axis=1))
        d_both[duo] = jnp.concatenate(d_rows, axis=0)

    def d_mix_stage(duo):
        d_mix[duo] = dot(vals[duo], d_both[duo], NT)
        d_proj[:, key_cols + duo * duo_vals:key_cols + (duo + 1) * duo_vals] = dot(mix[duo], d_both[duo], NN).astype(BF16)

    def d_key_stage(duo):
        d_scores = []
        for m in range(2):
            inner = jnp.sum(d_mix[duo] * probs[duo, m], axis=0, keepdims=True)
            d_score = probs[duo, m] * (d_mix[duo] - inner)
            d_scores.append((d_score if m == 0 else -lam[duo] * d_score).astype(BF16))
        d_proj[:, key_at[duo]] = dot(
            jnp.concatenate(d_scores, axis=1), spread[duo], NN
        ).astype(BF16)

    stages = (score_stage, softmax_stage, heads_stage, norm_stage, d_mix_stage, d_key_stage)
    for step in range(len(duos) + len(stages) - 1):
        for behind, stage in enumerate(stages):
            if step - behind in duos:
                stage(step - behind)
    half_width = width // 2
    at = pl.ds(pl.multiple_of((1 - half) * half_width, half_width), half_width)
    sent[...] = back_projected(d_proj, weights, at, key_cols).astype(BF16)


def back_projected(d_proj, weights, at, key_cols):
    return dot(d_proj[:, :key_cols], weights[0, at, :], NT) + dot(d_proj[:, key_cols:], weights[1, at, :], NT)


def query_mask(tokens, head_dim):
    row = np.arange(4 * tokens)[:, None]
    m, p = row // (2 * tokens), row // tokens % 2
    lane = np.arange(4 * head_dim)[None] // head_dim
    return jnp.asarray(np.where(lane == 2 * p + m, head_dim ** (-0.5), 0.0), BF16)


def one_group(info, lambdas, states, weights, mask, queries, cotangents, gain, *, group, query_at, token_at, tokens):
    rows, width = states.shape[2:]
    val_cols = gain.shape[1]
    pairs = lambdas.shape[0]
    head_dim = mask.shape[1] // 4
    key_cols = 2 * pairs * head_dim
    vmem = pl.BlockSpec(memory_space=pltpu.VMEM)
    smem = pl.BlockSpec(memory_space=pltpu.SMEM)
    kernel = functools.partial(
        group_kernel, group=group, query_at=query_at, token_at=token_at, pairs=pairs, head_dim=head_dim,
        value_dim=val_cols // pairs, tokens=tokens,
    )
    flops = 3 * rows * width * (key_cols + val_cols) + 14 * rows * tokens * val_cols
    return pl.pallas_call(
        kernel,
        out_shape=(
            jax.ShapeDtypeStruct((tokens, val_cols), BF16),
            jax.ShapeDtypeStruct((rows, width // 2), BF16),
            jax.ShapeDtypeStruct((rows, key_cols + val_cols), BF16),
        ),
        in_specs=[smem, smem, vmem, vmem, vmem, vmem, vmem, vmem],
        out_specs=(vmem, vmem, vmem),
        compiler_params=pltpu.CompilerParams(vmem_limit_bytes=12 * 1024 * 1024),
        cost_estimate=pl.CostEstimate(
            flops=4 * flops, bytes_accessed=6 * 1024 * 1024, transcendentals=2 * rows * tokens * pairs
        ),
    )(info, lambdas, states, weights, mask, queries, cotangents, gain)


def own_half_kernel(info, weights, *refs, count, key_cols):
    d_proj, received, (d_neigh, share) = refs[:count], refs[count:2 * count - 1], refs[2 * count - 1:]
    width = share.shape[1]
    at = pl.ds(pl.multiple_of(info[4] * width, width), width)
    for group in range(count - 1):
        @pl.when(pl.program_id(0) == group)
        def _():
            if group == 0:
                share[...] = back_projected(d_proj[count - 1], weights, at, key_cols)
            d_neigh[0, 0] = back_projected(d_proj[group], weights, at, key_cols) + received[group][...].astype(F32)


def own_half(info, weights, d_proj, received, order):
    count = len(d_proj)
    rows, width = received[0].shape
    vmem = pl.BlockSpec(memory_space=pltpu.VMEM)

    def place(step):
        group = 0
        for index, value in enumerate(order):
            group = jnp.where(step == index, value, group)
        return 0, group, 0, 0

    return pl.pallas_call(
        functools.partial(own_half_kernel, count=count, key_cols=weights.shape[2]),
        grid=(count - 1,),
        out_shape=(jax.ShapeDtypeStruct((1, count, rows, width), F32), jax.ShapeDtypeStruct((rows, width), F32)),
        in_specs=[pl.BlockSpec(memory_space=pltpu.SMEM)] + [vmem] * (2 * count),
        out_specs=(pl.BlockSpec((1, 1, rows, width), place), vmem),
        compiler_params=pltpu.CompilerParams(vmem_limit_bytes=12 * 1024 * 1024),
        cost_estimate=pl.CostEstimate(flops=2 * count * rows * width * 2048, bytes_accessed=6 * 1024 * 1024, transcendentals=0),
    )(info, weights, *d_proj, *received)


def last_sum_kernel(share, received, earlier, d_neigh):
    del earlier
    d_neigh[0, 0] = share[...] + received[...].astype(F32)


def last_sum(share, received, d_neigh, group):
    rows, width = share.shape
    vmem = pl.BlockSpec(memory_space=pltpu.VMEM)
    return pl.pallas_call(
        last_sum_kernel,
        grid=(1,),
        out_shape=jax.ShapeDtypeStruct(d_neigh.shape, F32),
        in_specs=[vmem, vmem, pl.BlockSpec(memory_space=pl.ANY)],
        out_specs=pl.BlockSpec((1, 1, rows, width), lambda step: (0, group, 0, 0)),
        input_output_aliases={2: 0},
        compiler_params=pltpu.CompilerParams(vmem_limit_bytes=6 * 1024 * 1024),
    )(share, received, d_neigh)


def swap(value, axis, flip):
    count = lax.axis_size(axis)
    return lax.ppermute(value, axis, [(i, i ^ flip) for i in range(count)])


def gather_weights(info, w_key, w_value, prepare, raw):
    core = lax.axis_index("seq") & 1
    first = core == 0
    own = jnp.where(first, w_key, w_value)
    got = lax.ppermute(jnp.where(first, w_value, w_key), "seq", other_core())
    rows = jnp.where(first, jnp.concatenate([own, got], axis=0), jnp.concatenate([got, own], axis=0))[None]
    for flip in (1, 3):
        rows = jnp.concatenate([rows, swap(rows, "grp", flip)], axis=0)
    steps = RELATIVE[1:]
    early = [lax.ppermute(rows, "seq", along(True, step)) for step in steps]
    straight = [lax.ppermute(rows, "seq", along(False, step)) for step in steps]
    block = jnp.concatenate(early, axis=0)
    block, raw = lax.optimization_barrier((block, raw))
    late = [lax.ppermute(block, "seq", along(False, step)) for step in steps]
    late[-1], ready = lax.optimization_barrier((late[-1], prepare(*raw)))
    pieces = [jnp.concatenate([rows] + straight, axis=0), block] + late
    places = [[(0, step) for step in RELATIVE]] + [[(step, to) for step in steps] for to in RELATIVE]
    swapped = [lax.ppermute(piece, "seq", other_core()) for piece in pieces]
    order = [(0, place) for place in places] + [(1, place) for place in places]
    return assemble(info, pieces + swapped, order), ready


def on_device(queries, neighbours, w_key, w_value, lambdas, gain, counts, d_out):
    group_count = neighbours.shape[1]
    group_len = queries.shape[1] // group_count
    cols = queries.shape[2]
    head_dim = w_key.shape[1] // (2 * lambdas.shape[0])
    seq_count = lax.axis_size("seq")
    seq = lax.axis_index("seq")
    last = group_count - 1
    info = jnp.stack([
        lax.axis_index("grp"), lax.div(seq, 2 * SIDE), lax.rem(lax.div(seq, 2), SIDE), seq & 1, lax.axis_index("mp"),
        seq * group_count, counts[0],
    ]).astype(jnp.int32)

    def prepare(queries, d_out, gain):
        first_tokens = jnp.concatenate([queries[0, :group_len], d_out[0, :group_len]], axis=1)
        return first_tokens, gain[None]

    weights, (first_tokens, gains) = gather_weights(
        info, w_key, w_value, prepare, (queries, d_out, gain)
    )
    coming = lax.ppermute(first_tokens, "seq", [(i, i - 1) for i in range(1, seq_count)])
    mask = query_mask(group_len, head_dim)
    attended, d_proj, received = [None] * group_count, [], []
    order = list(range(last - 1)) + [last, last - 1]
    turn = info
    for group in order:
        if group < last:
            own_rows = slice((group + 1) * group_len, (group + 2) * group_len)
            tokens_in = (queries, d_out)
            places = dict(query_at=(0, own_rows), token_at=(0, own_rows))
        else:
            tokens_in = (coming, coming)
            places = dict(query_at=(slice(None), slice(0, cols)), token_at=(slice(None), slice(cols, 2 * cols)))
        attended[group], sent, d_columns = one_group(
            turn, lambdas, neighbours, weights, mask, *tokens_in, gains, group=group, tokens=group_len, **places
        )
        d_proj.append(d_columns)
        received.append(swap(sent, "mp", 1))
        turn, d_proj[-1], coming = lax.optimization_barrier((turn, d_proj[-1], coming))
    first = lax.ppermute(attended[last], "seq", [(i, i + 1) for i in range(seq_count - 1)])
    d_neigh, share = own_half(info, weights, d_proj, received[:last], order)
    d_neigh = last_sum(share, received[last], d_neigh, order[last])
    return (jnp.concatenate([first] + attended[:last], axis=0)[None], d_neigh)


def solution(mesh):
    in_specs = (
        P("grp", "seq", "mp"),
        P("grp", "seq", None, None),
        P(("grp", "seq"), "mp"),
        P(("grp", "seq"), "mp"),
        P("mp"),
        P("mp"),
        P("grp"),
        P("grp", "seq", "mp"),
    )
    out_specs = (P("grp", "seq", "mp"), P("grp", "seq", None, "mp"))
    return jax.shard_map(
        on_device, mesh=mesh, in_specs=in_specs, out_specs=out_specs, check_vma=False
    )
```
